32 devices in a mesh: groups: 2 (over x), rep: 16 (over z, y, core).
Axes of the slice: x: 2, y: 2, z: 4, core: 2. Of those that a mesh axis runs over, the one named last changes fastest.
Arguments:
- tokens: bfloat16 [4096, 4096], P(('groups', 'rep')), parts along dimension 0, may hold values from -6 to 6
- cotangent: bfloat16 [4096, 11008], P(('groups', 'rep')), parts along dimension 0, may hold values from -0.4375 to 0.4375
- basis: bfloat16 [4096, 1024], P('rep'), may hold values from -0.09375 to 0.09375
- moment: float32 [1024, 11008], P(None, 'rep'), may hold values from -1.5 to 1.5
- second_moment: float32 [1024, 11008], P(None, 'rep'), may hold values from 0.002 to 0.05
Outputs:
- update: bfloat16 [8192, 11008], P(('groups', 'rep')), parts along dimension 0
- moment_next: float32 [2048, 11008], P('groups', 'rep'), parts along dimension 0
- second_next: float32 [2048, 11008], P('groups', 'rep'), parts along dimension 0
The draws below stay inside these ranges and needn't reach their ends.
There are 2 independent parts, one for each index of `groups`. The reference program is written for one: setup_inputs(seed, part) draws one part's arguments, and reference() takes and returns one part's arrays. A program takes and returns all parts, laid end to end along the dimension named above; an argument that names none is the same for every part. Nothing has to cross between parts.
All inputs are finite; a program needn't handle non-finite values.
Results may differ from the reference program's by a relative error of at most 0.0055.
Values may be sent and summed in bfloat16 or wider, within the bound.
A program may use at most 128 MiB of HBM per device.

```python
import math
import jax
import jax.numpy as jnp

D = 4096
FF = 11008
RANK = 1024
TOKENS = 2048


def strengthened(result, stream_key, source, target, shards_of, factor):
    def block_of(axis_at):
        return (jnp.arange(result.shape[axis_at]) // (result.shape[axis_at] // shards_of)).reshape((-1,) + (1,) * (result.ndim - 1 - axis_at))

    near = jax.random.permutation(stream_key, shards_of)[block_of(target)]
    far = (block_of(target) + shards_of // 2) % shards_of
    return jnp.where((block_of(source) == near) | (block_of(source) == far), factor * result, result)


def steps_of(own_key, shape, split, low, high):
    gain = 1.0
    for dim, parts in split:
        heights = jax.random.uniform(jax.random.fold_in(jax.random.fold_in(own_key, 6), dim), (parts,), jnp.float32, low / len(split), high / len(split))
        gain = gain * jnp.repeat(jnp.exp(heights), shape[dim] // parts).reshape((-1,) + (1,) * (len(shape) - 1 - dim))
    return gain


def centred(rng, dims, spread, bound, cuts=(), kind=jnp.bfloat16):
    factor_of = steps_of(rng, dims, cuts, -0.22, 0.18) if cuts else 1.0
    result = jax.random.normal(rng, dims, jnp.float32) * spread * factor_of
    return jnp.minimum(jnp.maximum(result, -bound), bound).astype(kind)


def bell_draw_with(rng, dims, spread, limit, pieces, heavy, held_as=jnp.bfloat16):
    values = spread * jax.random.normal(rng, dims, jnp.float32)
    if pieces:
        values = values * steps_of(rng, dims, pieces, -0.22, 0.18)
    return jnp.clip(strengthened(values, jax.random.fold_in(rng, 3), *heavy), -limit, limit).astype(held_as)


def setup_inputs(seed: int = 0, part: int = 0) -> dict:
    seeds = jax.random.split(jax.random.key(seed), 6)
    own_keys = jax.random.split(jax.random.fold_in(seeds[5], part), 6)
    return {
        "tokens": centred(own_keys[0], (TOKENS, D), 1.0, 6.0, ((0, 16),)),
        "cotangent": bell_draw_with(own_keys[1], (TOKENS, FF), (TOKENS ** -0.5), 0.4375, ((0, 16),), (0, 1, 16, 2.0)),
        "basis": centred(seeds[2], (D, RANK), D ** -0.5, 0.09375, ((0, 16),)),
        "moment": centred(seeds[3], (RANK, FF), 0.1, 1.5, ((1, 16),), jnp.float32),
        "second_moment": jnp.clip(jnp.exp(math.log(0.05) - 3.218876 * jax.random.uniform(seeds[4], (RANK, FF), jnp.float32) ** steps_of(seeds[4], (RANK, FF), ((1, 16),), -0.2, 0.2)), 0.002, 0.05),
    }


def reference(tokens, cotangent, basis, moment, second_moment):
    projected = jnp.dot(tokens, basis, preferred_element_type=jnp.float32).astype(jnp.bfloat16)
    low_grad = jnp.dot(projected.T, cotangent, preferred_element_type=jnp.float32)
    moment_next = 0.9 * moment + 0.1 * low_grad
    second_next = 0.999 * second_moment + 0.001 * low_grad * low_grad
    ratio = (moment_next / (jnp.sqrt(second_next) + 1e-08)).astype(jnp.bfloat16)
    update = jnp.dot(basis, ratio, preferred_element_type=jnp.float32).astype(jnp.bfloat16)
    return (update, moment_next, second_next)
```

```python
import functools

import jax
import jax.numpy as jnp
from jax import lax
from jax.experimental import pallas as pl
from jax.experimental.pallas import tpu as pltpu
from jax.sharding import PartitionSpec as P

CORES = 2
NT = (((1,), (1,)), ((), ()))


def kernel(
    n, Z, Y, tokens_hbm, ct_hbm, basis_hbm, moment_hbm, second_hbm,
    out_hbm, moment_out, second_out,
    tok, ball, pacc, ptall, ctall, mom, sec, rt, ubuf,
    lsem, asem, bsem, psem, csem_s, csem_r, usem_s, usem_r, rsem,
):
    me = lax.axis_index("rep")
    z = me // (Y * CORES)
    y = (me // CORES) % Y
    c = me % CORES
    rows = basis_hbm.shape[0]
    T = tokens_hbm.shape[0]
    rank = basis_hbm.shape[1]

    def dev(zz, yy, cc):
        return (zz * Y + yy) * CORES + cc

    barrier = pltpu.get_barrier_semaphore()

    @pl.loop(1, n)
    def _(k):
        pl.semaphore_signal(
            barrier, inc=1, device_id={"rep": (me + k) % n},
            device_id_type=pl.DeviceIdType.MESH,
        )

    def local(src, dst, i):
        return pltpu.make_async_copy(src, dst, lsem.at[i])

    def remote(src, dst, ss, rs, to):
        return pltpu.make_async_remote_copy(
            src_ref=src, dst_ref=dst, send_sem=ss, recv_sem=rs,
            device_id={"rep": to}, device_id_type=pl.DeviceIdType.MESH,
        )

    def bas(b):
        return ball.at[pl.ds(pl.multiple_of(b * rows, 16), rows), :]

    def pro(b):
        return ptall.at[:, pl.ds(pl.multiple_of(b * T, 128), T)]

    def cot(b):
        return ctall.at[:, pl.ds(pl.multiple_of(b * T, 128), T)]

    own = local(basis_hbm, bas(me), 0)
    own.start()
    load_tok = local(tokens_hbm, tok, 1)
    load_tok.start()
    load_mom = local(moment_hbm, mom, 2)
    load_mom.start()
    load_sec = local(second_hbm, sec, 3)
    load_sec.start()
    own_ct = local(ct_hbm.at[me], cot(me), 4)
    own_ct.start()
    own.wait()
    pl.semaphore_wait(barrier, n - 1)

    def up(blk, S, zs):
        b = blk(dev(zs, y, c))
        return remote(b, b, S.at[0, zs], S.at[5, zs], dev((z + 1) % Z, y, c))

    def down(blk, S, zs):
        b = blk(dev(zs, y, c))
        return remote(b, b, S.at[1, zs], S.at[5, zs], dev((z + Z - 1) % Z, y, c))

    def across(blk, S, zs, recv=False):
        b = blk(dev(zs, (y + 1) % Y if recv else y, c))
        return remote(b, b, S.at[2, zs], S.at[6, zs], dev(z, (y + 1) % Y, c))

    def core(blk, S, zs, ys, recv=False):
        b = blk(dev(zs, ys, (c + 1) % CORES if recv else c))
        i = (ys + Y - y) % Y
        return remote(b, b, S.at[3 + i, zs], S.at[7 + ys, zs], dev(z, y, (c + 1) % CORES))

    def spread(blk, S, zs):
        if Y > 1:
            across(blk, S, zs).start()
        core(blk, S, zs, y).start()

    def both(k, f):
        @pl.when(z - k >= 0)
        def _():
            f(z - k, True)

        @pl.when(z + k < Z)
        def _():
            f(z + k, False)

    def line_start(blk, S):
        @pl.when(z + 1 < Z)
        def _():
            up(blk, S, z).start()

        @pl.when(z >= 1)
        def _():
            down(blk, S, z).start()

    def line_take(blk, S, zs, below):
        up(blk, S, zs).wait_recv()
        if below:
            @pl.when(z + 1 < Z)
            def _():
                up(blk, S, zs).start()
        else:
            @pl.when(z >= 1)
            def _():
                down(blk, S, zs).start()

    def line_sent(blk, S):
        @pl.loop(0, Z)
        def _(zs):
            @pl.when((zs <= z) & (z + 1 < Z))
            def _():
                up(blk, S, zs).wait_send()

            @pl.when((zs >= z) & (z >= 1))
            def _():
                down(blk, S, zs).wait_send()

    def gather(blk, S, middle=None):
        def crossed(zs, _=None):
            if Y > 1:
                across(blk, S, zs, recv=True).wait_recv()
                core(blk, S, zs, (y + 1) % Y).start()

        def arrived(zs, below):
            line_take(blk, S, zs, below)
            spread(blk, S, zs)

        line_start(blk, S)
        spread(blk, S, z)

        @pl.loop(1, Z)
        def _(k):
            both(k, arrived)

            @pl.when(k == 1)
            def _():
                crossed(z)

            @pl.when(k > 1)
            def _():
                both(k - 1, crossed)

        if middle is not None:
            middle()
        both(Z - 1, crossed)

        @pl.loop(0, Z)
        def _(zs):
            for ys in range(Y):
                core(blk, S, zs, ys, recv=True).wait_recv()

    def gather_sent(blk, S):
        line_sent(blk, S)

        @pl.loop(0, Z)
        def _(zs):
            if Y > 1:
                across(blk, S, zs).wait_send()
            for ys in range(Y):
                core(blk, S, zs, ys).wait_send()

    def cot_copy(k):
        to = (me + k) % n
        return remote(ct_hbm.at[to], cot(me), csem_s.at[k], csem_r.at[me], to)

    def cot_start():
        @pl.loop(1, n)
        def _(k):
            cot_copy(k).start()

    gather(bas, bsem, cot_start)

    load_tok.wait()
    pacc[...] = jnp.zeros_like(pacc)
    step = 512

    @pl.loop(0, ball.shape[0] // step)
    def _(k):
        at = pl.ds(pl.multiple_of(k * step, step), step)
        pacc[...] += jnp.dot(tok[:, at], ball[at, :], preferred_element_type=jnp.float32)

    pro(me)[...] = pacc[...].T.astype(jnp.bfloat16)
    gather(pro, psem)

    @pl.loop(1, n)
    def _(k):
        src = (me + k) % n
        remote(cot(src), cot(src), csem_s.at[k], csem_r.at[src], src).wait_recv()

    own_ct.wait()
    load_mom.wait()
    load_sec.wait()

    def adam_copy(i, r):
        src, dst = ((mom, moment_out), (sec, second_out))[i]
        at = pl.ds(pl.multiple_of(r * 128, 128), 128)
        return pltpu.make_async_copy(src.at[at, :], dst.at[at, :], asem.at[i, r])

    @pl.loop(0, rank // 128)
    def _(r):
        at = pl.ds(pl.multiple_of(r * 128, 128), 128)
        low = lax.dot_general(ptall[at, :], ctall[...], NT, preferred_element_type=jnp.float32)
        moment_next = 0.9 * mom[at, :] + 0.1 * low
        second_next = 0.999 * sec[at, :] + 0.001 * low * low
        mom[at, :] = moment_next
        sec[at, :] = second_next
        ratio = moment_next / (jnp.sqrt(second_next) + 1e-08)
        rt[z, :, at] = ratio.T.astype(jnp.bfloat16)
        adam_copy(0, r).start()
        adam_copy(1, r).start()

    def rat(b):
        return rt.at[b // (Y * CORES)]

    planes = Y * CORES

    def u_copy(p, zs, recv=False):
        b = dev(zs, 0, 0) + (p if recv else me % planes)
        src = ubuf.at[p, zs]
        return remote(src, out_hbm.at[b], usem_s.at[p, zs], usem_r.at[p if recv else me % planes, zs], z * planes + p)

    def u_local(zs):
        q = me % planes
        return pltpu.make_async_copy(ubuf.at[q, zs], out_hbm.at[dev(zs, y, c)], usem_s.at[q, zs])

    def expand(zs):
        for i in range(planes):
            p = (me + i + 1) % planes
            at = pl.ds(pl.multiple_of((z * planes + p) * rows, 16), rows)
            ubuf[p, zs] = lax.dot_general(
                ball[at, :], rt[zs], NT, preferred_element_type=jnp.float32
            ).astype(jnp.bfloat16)
            if i < planes - 1:
                u_copy(p, zs).start()
            else:
                u_local(zs).start()

    def ratio_arrived(zs, below):
        line_take(rat, rsem, zs, below)
        expand(zs)

    line_start(rat, rsem)
    expand(z)

    @pl.loop(1, Z)
    def _(k):
        both(k, ratio_arrived)

    gather_sent(bas, bsem)
    gather_sent(pro, psem)
    line_sent(rat, rsem)

    @pl.loop(1, n)
    def _(k):
        cot_copy(k).wait_send()

    @pl.loop(0, rank // 128)
    def _(r):
        adam_copy(0, r).wait()
        adam_copy(1, r).wait()

    @pl.loop(0, Z)
    def _(zs):
        for i in range(1, planes):
            p = (me + i) % planes
            u_copy(p, zs).wait_send()
            u_copy(p, zs, recv=True).wait_recv()
        u_local(zs).wait()


def on_device(n, Z, Y, tokens, cotangent, basis, moment, second_moment):
    T, D = tokens.shape
    rows, rank = basis.shape
    width = moment.shape[1]
    bf = jnp.bfloat16
    ct = cotangent.T.reshape(n, width, T)
    any_spec = pl.BlockSpec(memory_space=pl.ANY)
    dma = pltpu.SemaphoreType.DMA
    out, moment_next, second_next = pl.pallas_call(
        functools.partial(kernel, n, Z, Y),
        out_shape=(
            jax.ShapeDtypeStruct((n, rows, width), bf),
            jax.ShapeDtypeStruct(moment.shape, jnp.float32),
            jax.ShapeDtypeStruct(moment.shape, jnp.float32),
        ),
        in_specs=[any_spec] * 5,
        out_specs=(any_spec,) * 3,
        scratch_shapes=[
            pltpu.VMEM((T, D), bf),
            pltpu.VMEM((D, rank), bf),
            pltpu.VMEM((T, rank), jnp.float32),
            pltpu.VMEM((rank, n * T), bf),
            pltpu.VMEM((width, n * T), bf),
            pltpu.VMEM((rank, width), jnp.float32),
            pltpu.VMEM((rank, width), jnp.float32),
            pltpu.VMEM((Z, width, rank), bf),
            pltpu.VMEM((Y * CORES, Z, rows, width), bf),
            dma((5,)),
            dma((2, rank // 128)),
            dma((7 + Y, Z)),
            dma((7 + Y, Z)),
            dma((n,)),
            dma((n,)),
            dma((Y * CORES, Z)),
            dma((Y * CORES, Z)),
            dma((6, Z)),
        ],
        compiler_params=pltpu.CompilerParams(
            collective_id=0, has_side_effects=True, vmem_limit_bytes=60 * 2**20
        ),
        cost_estimate=pl.CostEstimate(
            flops=2 * T * rank * (D + n * width) + 2 * rank * rows * n * width,
            bytes_accessed=4 * D * rank, transcendentals=rank * width,
        ),
    )(tokens, ct, basis, moment, second_moment)
    update = jnp.transpose(out, (1, 0, 2)).reshape(rows, n * width)
    return (update, moment_next, second_next)


def solution(mesh):
    n = mesh.shape["rep"]
    Y = max(1, 4 // mesh.shape["groups"])
    Z = n // (Y * CORES)
    in_specs = (
        P(("groups", "rep"), None),
        P(("groups", "rep"), None),
        P("rep", None),
        P(None, "rep"),
        P(None, "rep"),
    )
    out_specs = (P(("groups", "rep"), None), P("groups", "rep"), P("groups", "rep"))
    return jax.shard_map(
        functools.partial(on_device, n, Z, Y),
        mesh=mesh, in_specs=in_specs, out_specs=out_specs, check_vma=False,
    )
```

```python
import functools

import jax
import jax.numpy as jnp
from jax import lax
from jax.experimental import pallas as pl
from jax.experimental.pallas import tpu as pltpu
from jax.sharding import PartitionSpec as P

CORES = 2
NT = (((1,), (1,)), ((), ()))


def parts_of(width):
    if width % 16:
        return ((0, width),)
    half = (width // 2 + 15) // 16 * 16
    return ((0, half), (half, width - half))


def kernel(
    n, Z, Y, tokens_hbm, ct_hbm, basis_hbm, moment_hbm, second_hbm,
    out_hbm, moment_out, second_out,
    tok, ball, pacc, ptall, ctall, mom, sec, rt, ubuf,
    lsem, asem, bsem, psem, csem_s, csem_r, usem_s, usem_r, rsem,
):
    me = lax.axis_index("rep")
    z = me // (Y * CORES)
    y = (me // CORES) % Y
    c = me % CORES
    rows = basis_hbm.shape[0]
    T = tokens_hbm.shape[0]
    rank = basis_hbm.shape[1]
    parts = parts_of(moment_hbm.shape[0])
    R = len(parts)

    def dev(zz, yy, cc):
        return (zz * Y + yy) * CORES + cc

    barrier = pltpu.get_barrier_semaphore()

    @pl.loop(1, n)
    def _(k):
        pl.semaphore_signal(
            barrier, inc=1, device_id={"rep": (me + k) % n},
            device_id_type=pl.DeviceIdType.MESH,
        )

    def local(src, dst, i):
        return pltpu.make_async_copy(src, dst, lsem.at[i])

    def remote(src, dst, ss, rs, to):
        return pltpu.make_async_remote_copy(
            src_ref=src, dst_ref=dst, send_sem=ss, recv_sem=rs,
            device_id={"rep": to}, device_id_type=pl.DeviceIdType.MESH,
        )

    def bas(b):
        return ball.at[pl.ds(pl.multiple_of(b * rows, 16), rows), :]

    def pro(b):
        return ptall.at[pl.ds(pl.multiple_of(b * T, 128), T), :]

    def cot(b):
        return ctall.at[:, pl.ds(pl.multiple_of(b * T, 128), T)]

    own = local(basis_hbm, bas(me), 0)
    own.start()
    load_tok = local(tokens_hbm, tok, 1)
    load_tok.start()
    load_mom = local(moment_hbm, mom, 2)
    load_mom.start()
    load_sec = local(second_hbm, sec, 3)
    load_sec.start()
    own_ct = local(ct_hbm.at[me], cot(me), 4)
    own_ct.start()
    own.wait()
    pl.semaphore_wait(barrier, n - 1)

    def up(blk, S, zs, *j):
        b = blk(dev(zs, y, c), *j)
        i = zs * R + j[0] if j else zs
        return remote(b, b, S.at[0, i], S.at[5, i], dev((z + 1) % Z, y, c))

    def down(blk, S, zs, *j):
        b = blk(dev(zs, y, c), *j)
        i = zs * R + j[0] if j else zs
        return remote(b, b, S.at[1, i], S.at[5, i], dev((z + Z - 1) % Z, y, c))

    def across(blk, S, zs, recv=False):
        b = blk(dev(zs, (y + 1) % Y if recv else y, c))
        return remote(b, b, S.at[2, zs], S.at[6, zs], dev(z, (y + 1) % Y, c))

    def core(blk, S, zs, ys, recv=False):
        b = blk(dev(zs, ys, (c + 1) % CORES if recv else c))
        i = (ys + Y - y) % Y
        return remote(b, b, S.at[3 + i, zs], S.at[7 + ys, zs], dev(z, y, (c + 1) % CORES))

    def spread(blk, S, zs):
        if Y > 1:
            across(blk, S, zs).start()
        core(blk, S, zs, y).start()

    def both(k, f):
        @pl.when(z - k >= 0)
        def _():
            f(z - k, True)

        @pl.when(z + k < Z)
        def _():
            f(z + k, False)

    def line_start(blk, S, *j):
        @pl.when(z + 1 < Z)
        def _():
            up(blk, S, z, *j).start()

        @pl.when(z >= 1)
        def _():
            down(blk, S, z, *j).start()

    def line_take(blk, S, zs, below, *j):
        up(blk, S, zs, *j).wait_recv()
        if below:
            @pl.when(z + 1 < Z)
            def _():
                up(blk, S, zs, *j).start()
        else:
            @pl.when(z >= 1)
            def _():
                down(blk, S, zs, *j).start()

    def line_sent(blk, S, *j):
        @pl.loop(0, Z)
        def _(zs):
            @pl.when((zs <= z) & (z + 1 < Z))
            def _():
                up(blk, S, zs, *j).wait_send()

            @pl.when((zs >= z) & (z >= 1))
            def _():
                down(blk, S, zs, *j).wait_send()

    def gather(blk, S, middle=None):
        def crossed(zs, _=None):
            if Y > 1:
                across(blk, S, zs, recv=True).wait_recv()
                core(blk, S, zs, (y + 1) % Y).start()

        def arrived(zs, below):
            line_take(blk, S, zs, below)
            spread(blk, S, zs)

        line_start(blk, S)
        spread(blk, S, z)

        @pl.loop(1, Z)
        def _(k):
            both(k, arrived)

        if middle is not None:
            middle()
        crossed(z)

        @pl.loop(1, Z)
        def _(k):
            both(k, crossed)

        @pl.loop(0, Z)
        def _(zs):
            for ys in range(Y):
                core(blk, S, zs, ys, recv=True).wait_recv()

    def gather_sent(blk, S):
        line_sent(blk, S)

        @pl.loop(0, Z)
        def _(zs):
            if Y > 1:
                across(blk, S, zs).wait_send()
            for ys in range(Y):
                core(blk, S, zs, ys).wait_send()

    def cot_copy(k):
        to = (me + k) % n
        return remote(ct_hbm.at[to], cot(me), csem_s.at[k], csem_r.at[me], to)

    def cot_start():
        @pl.loop(1, n)
        def _(k):
            cot_copy(k).start()

    gather(bas, bsem, cot_start)

    load_tok.wait()
    pacc[...] = jnp.zeros_like(pacc)
    step = 512

    @pl.loop(0, ball.shape[0] // step)
    def _(k):
        at = pl.ds(pl.multiple_of(k * step, step), step)
        pacc[...] += jnp.dot(tok[:, at], ball[at, :], preferred_element_type=jnp.float32)

    pro(me)[...] = pacc[...].astype(jnp.bfloat16)
    gather(pro, psem)

    @pl.loop(1, n)
    def _(k):
        src = (me + k) % n
        remote(cot(src), cot(src), csem_s.at[k], csem_r.at[src], src).wait_recv()

    own_ct.wait()
    load_mom.wait()
    load_sec.wait()

    def adam_copy(i, j):
        src, dst = ((mom, moment_out), (sec, second_out))[i]
        at = pl.ds(*parts[j])
        return pltpu.make_async_copy(src.at[at, :], dst.at[at, :], asem.at[i, j])

    def rat(b, j):
        return rt.at[b // (Y * CORES), pl.ds(*parts[j]), :]

    planes = Y * CORES

    def u_copy(p, zs, j, recv=False):
        at = pl.ds(*parts[j])
        b = dev(zs, 0, 0) + (p if recv else me % planes)
        i = zs * R + j
        return remote(
            ubuf.at[p, zs, at, :], out_hbm.at[b, at, :], usem_s.at[p, i],
            usem_r.at[p if recv else me % planes, i], z * planes + p,
        )

    def u_local(zs, j):
        at = pl.ds(*parts[j])
        q = me % planes
        return pltpu.make_async_copy(
            ubuf.at[q, zs, at, :], out_hbm.at[dev(zs, y, c), at, :], usem_s.at[q, zs * R + j]
        )

    def expand(zs, j):
        part = pl.ds(*parts[j])
        for i in (1, 2, 0, 3) if planes == 4 else range(planes):
            p = (me + i + 1) % planes
            at = pl.ds(pl.multiple_of((z * planes + p) * rows, 16), rows)
            ubuf[p, zs, part, :] = lax.dot_general(
                rt[zs, part, :], ball[at, :], NT, preferred_element_type=jnp.float32
            ).astype(jnp.bfloat16)
            if i < planes - 1:
                u_copy(p, zs, j).start()
            else:
                u_local(zs, j).start()

    for j in range(R):
        at = pl.ds(*parts[j])
        low = jnp.dot(ctall[at, :], ptall[...], preferred_element_type=jnp.float32)
        moment_next = 0.9 * mom[at, :] + 0.1 * low
        second_next = 0.999 * sec[at, :] + 0.001 * low * low
        mom[at, :] = moment_next
        sec[at, :] = second_next
        ratio = moment_next / (jnp.sqrt(second_next) + 1e-08)
        rt[z, at, :] = ratio.astype(jnp.bfloat16)
        line_start(rat, rsem, j)
        adam_copy(0, j).start()
        adam_copy(1, j).start()

    for j in range(R):
        expand(z, j)

    @pl.loop(1, Z)
    def _(k):
        for j in range(R):
            both(k, lambda zs, below: line_take(rat, rsem, zs, below, j))
            both(k, lambda zs, below: expand(zs, j))

    gather_sent(bas, bsem)
    gather_sent(pro, psem)
    for j in range(R):
        line_sent(rat, rsem, j)

    @pl.loop(1, n)
    def _(k):
        cot_copy(k).wait_send()

    for j in range(R):
        adam_copy(0, j).wait()
        adam_copy(1, j).wait()

    @pl.loop(0, Z)
    def _(zs):
        for j in range(R):
            for i in range(1, planes):
                p = (me + i) % planes
                u_copy(p, zs, j).wait_send()
                u_copy(p, zs, j, recv=True).wait_recv()
            u_local(zs, j).wait()


def on_device(n, Z, Y, tokens, cotangent, basis, moment, second_moment):
    T, D = tokens.shape
    rows, rank = basis.shape
    width = moment.shape[1]
    R = len(parts_of(width))
    bf = jnp.bfloat16
    ct = cotangent.T.reshape(n, width, T)
    any_spec = pl.BlockSpec(memory_space=pl.ANY)
    dma = pltpu.SemaphoreType.DMA
    out, moment_next, second_next = pl.pallas_call(
        functools.partial(kernel, n, Z, Y),
        out_shape=(
            jax.ShapeDtypeStruct((n, width, rows), bf),
            jax.ShapeDtypeStruct((width, rank), jnp.float32),
            jax.ShapeDtypeStruct((width, rank), jnp.float32),
        ),
        in_specs=[any_spec] * 5,
        out_specs=(any_spec,) * 3,
        scratch_shapes=[
            pltpu.VMEM((T, D), bf),
            pltpu.VMEM((D, rank), bf),
            pltpu.VMEM((T, rank), jnp.float32),
            pltpu.VMEM((n * T, rank), bf),
            pltpu.VMEM((width, n * T), bf),
            pltpu.VMEM((width, rank), jnp.float32),
            pltpu.VMEM((width, rank), jnp.float32),
            pltpu.VMEM((Z, width, rank), bf),
            pltpu.VMEM((Y * CORES, Z, width, rows), bf),
            dma((5,)),
            dma((2, R)),
            dma((7 + Y, Z)),
            dma((7 + Y, Z)),
            dma((n,)),
            dma((n,)),
            dma((Y * CORES, Z * R)),
            dma((Y * CORES, Z * R)),
            dma((6, Z * R)),
        ],
        compiler_params=pltpu.CompilerParams(
            collective_id=0, has_side_effects=True, vmem_limit_bytes=60 * 2**20
        ),
        cost_estimate=pl.CostEstimate(
            flops=2 * T * rank * (D + n * width) + 2 * rank * rows * n * width,
            bytes_accessed=4 * D * rank, transcendentals=rank * width,
        ),
    )(tokens, ct, basis, moment.T, second_moment.T)
    update = out.reshape(n * width, rows).T
    return (update, moment_next.T, second_next.T)


def solution(mesh):
    n = mesh.shape["rep"]
    Y = max(1, 4 // mesh.shape["groups"])
    Z = n // (Y * CORES)
    in_specs = (
        P(("groups", "rep"), None),
        P(("groups", "rep"), None),
        P("rep", None),
        P(None, "rep"),
        P(None, "rep"),
    )
    out_specs = (P(("groups", "rep"), None), P("groups", "rep"), P("groups", "rep"))
    return jax.shard_map(
        functools.partial(on_device, n, Z, Y),
        mesh=mesh, in_specs=in_specs, out_specs=out_specs, check_vma=False,
    )
```

```python
import functools

import jax
import jax.numpy as jnp
from jax import lax
from jax.experimental import pallas as pl
from jax.experimental.pallas import tpu as pltpu
from jax.sharding import PartitionSpec as P

CORES = 2
BATCH = 2
NT = (((1,), (1,)), ((), ()))


def parts_of(width):
    if width % 16:
        return ((0, width),)
    part = (width // 4 + 15) // 16 * 16
    return tuple((i * part, min(part, width - i * part)) for i in range(4))


def kernel(
    n, Z, Y, tokens_hbm, ct_hbm, basis_hbm, moment_hbm, second_hbm,
    out_hbm, moment_out, second_out,
    tok, ball, pacc, ptall, ctall, mom, sec, rt, ubuf, cv, ctv,
    lsem, asem, bsem, psem, csem_s, csem_r, usem_s, usem_r, rsem,
):
    me = lax.axis_index("rep")
    z = me // (Y * CORES)
    y = (me // CORES) % Y
    c = me % CORES
    rows = basis_hbm.shape[0]
    T = tokens_hbm.shape[0]
    rank = basis_hbm.shape[1]
    parts = parts_of(moment_hbm.shape[0])
    R = len(parts)

    def dev(zz, yy, cc):
        return (zz * Y + yy) * CORES + cc

    barrier = pltpu.get_barrier_semaphore()

    @pl.loop(1, n)
    def _(k):
        pl.semaphore_signal(
            barrier, inc=1, device_id={"rep": (me + k) % n},
            device_id_type=pl.DeviceIdType.MESH,
        )

    def local(src, dst, i):
        return pltpu.make_async_copy(src, dst, lsem.at[i])

    def remote(src, dst, ss, rs, to):
        return pltpu.make_async_remote_copy(
            src_ref=src, dst_ref=dst, send_sem=ss, recv_sem=rs,
            device_id={"rep": to}, device_id_type=pl.DeviceIdType.MESH,
        )

    def bas(b):
        return ball.at[pl.ds(pl.multiple_of(b * rows, 16), rows), :]

    def pro(b):
        return ptall.at[pl.ds(pl.multiple_of(b * T, 128), T), :]

    def cot(b):
        return ctall.at[:, pl.ds(pl.multiple_of(b * T, 128), T)]

    own = local(basis_hbm, bas(me), 0)
    own.start()
    load_tok = local(tokens_hbm, tok, 1)
    load_tok.start()
    load_mom = local(moment_hbm, mom, 2)
    load_mom.start()
    load_sec = local(second_hbm, sec, 3)
    load_sec.start()
    B = min(BATCH, (n - 1) // max(Z - 1, 1))
    inside = ct_hbm.ndim == 2
    width = moment_hbm.shape[0]

    def ct_of(b):
        return ctv.at[pl.ds(pl.multiple_of(b * width, 16), width), :] if inside else ct_hbm.at[b]

    own_ct = local(ct_of(me), cot(me), 4)
    if inside:
        load_ct = local(ct_hbm, cv, 5)
        load_ct.start()
    else:
        own_ct.start()
    own.wait()
    pl.semaphore_wait(barrier, n - 1)

    def up(blk, S, zs, *j):
        b = blk(dev(zs, y, c), *j)
        i = zs * R + j[0] if j else zs
        return remote(b, b, S.at[0, i], S.at[5, i], dev((z + 1) % Z, y, c))

    def down(blk, S, zs, *j):
        b = blk(dev(zs, y, c), *j)
        i = zs * R + j[0] if j else zs
        return remote(b, b, S.at[1, i], S.at[5, i], dev((z + Z - 1) % Z, y, c))

    def across(blk, S, zs, recv=False):
        b = blk(dev(zs, (y + 1) % Y if recv else y, c))
        return remote(b, b, S.at[2, zs], S.at[6, zs], dev(z, (y + 1) % Y, c))

    def core(blk, S, zs, ys, recv=False):
        b = blk(dev(zs, ys, (c + 1) % CORES if recv else c))
        i = (ys + Y - y) % Y
        return remote(b, b, S.at[3 + i, zs], S.at[7 + ys, zs], dev(z, y, (c + 1) % CORES))

    def spread(blk, S, zs):
        if Y > 1:
            across(blk, S, zs).start()
        core(blk, S, zs, y).start()

    def both(k, f):
        @pl.when(z - k >= 0)
        def _():
            f(z - k, True)

        @pl.when(z + k < Z)
        def _():
            f(z + k, False)

    def line_start(blk, S, *j):
        @pl.when(z + 1 < Z)
        def _():
            up(blk, S, z, *j).start()

        @pl.when(z >= 1)
        def _():
            down(blk, S, z, *j).start()

    def line_take(blk, S, zs, below, *j):
        up(blk, S, zs, *j).wait_recv()
        if below:
            @pl.when(z + 1 < Z)
            def _():
                up(blk, S, zs, *j).start()
        else:
            @pl.when(z >= 1)
            def _():
                down(blk, S, zs, *j).start()

    def line_sent(blk, S, *j):
        @pl.loop(0, Z)
        def _(zs):
            @pl.when((zs <= z) & (z + 1 < Z))
            def _():
                up(blk, S, zs, *j).wait_send()

            @pl.when((zs >= z) & (z >= 1))
            def _():
                down(blk, S, zs, *j).wait_send()

    def gather(blk, S, early=None, middle=None, batch=None):
        def crossed(zs, _=None):
            if Y > 1:
                across(blk, S, zs, recv=True).wait_recv()
                core(blk, S, zs, (y + 1) % Y).start()

        def arrived(zs, below):
            line_take(blk, S, zs, below)
            spread(blk, S, zs)

        line_start(blk, S)
        spread(blk, S, z)
        if early is not None:
            early()

        @pl.loop(1, Z)
        def _(k):
            both(k, arrived)
            if batch is not None:
                batch(k)

        if middle is not None:
            middle()
        crossed(z)

        @pl.loop(1, Z)
        def _(k):
            both(k, crossed)

        @pl.loop(0, Z)
        def _(zs):
            for ys in range(Y):
                core(blk, S, zs, ys, recv=True).wait_recv()

    def gather_sent(blk, S):
        line_sent(blk, S)

        @pl.loop(0, Z)
        def _(zs):
            if Y > 1:
                across(blk, S, zs).wait_send()
            for ys in range(Y):
                core(blk, S, zs, ys).wait_send()

    def cot_copy(k):
        to = (me + k) % n
        return remote(ct_of(to), cot(me), csem_s.at[k], csem_r.at[me], to)

    def cot_start():
        @pl.loop(1 + (Z - 1) * B, n)
        def _(k):
            cot_copy(k).start()

    def cot_batch(k):
        for i in range(B):
            cot_copy((k - 1) * B + i + 1).start()

    def turn():
        if inside:
            load_ct.wait()

            @pl.loop(0, cv.shape[1] // 128)
            def _(k):
                at = pl.ds(pl.multiple_of(k * 128, 128), 128)
                ctv[at, :] = cv[:, at].T

            own_ct.start()

    gather(bas, bsem, turn, cot_start, cot_batch)

    load_tok.wait()
    pacc[...] = jnp.zeros_like(pacc)
    step = 512

    @pl.loop(0, ball.shape[0] // step)
    def _(k):
        at = pl.ds(pl.multiple_of(k * step, step), step)
        pacc[...] += jnp.dot(tok[:, at], ball[at, :], preferred_element_type=jnp.float32)

    pro(me)[...] = pacc[...].astype(jnp.bfloat16)
    gather(pro, psem)

    @pl.loop(1, n)
    def _(k):
        src = (me + k) % n
        remote(cot(src), cot(src), csem_s.at[k], csem_r.at[src], src).wait_recv()

    own_ct.wait()
    load_mom.wait()
    load_sec.wait()

    def adam_copy(i, j):
        src, dst = ((mom, moment_out), (sec, second_out))[i]
        at = pl.ds(*parts[j])
        return pltpu.make_async_copy(src.at[at, :], dst.at[at, :], asem.at[i, j])

    def rat(b, j):
        return rt.at[b // (Y * CORES), pl.ds(*parts[j]), :]

    planes = Y * CORES

    def u_copy(p, zs, j, recv=False):
        at = pl.ds(*parts[j])
        b = dev(zs, 0, 0) + (p if recv else me % planes)
        i = zs * R + j
        return remote(
            ubuf.at[p, zs, at, :], out_hbm.at[b, at, :], usem_s.at[p, i],
            usem_r.at[p if recv else me % planes, i], z * planes + p,
        )

    def u_local(zs, j):
        at = pl.ds(*parts[j])
        q = me % planes
        return pltpu.make_async_copy(
            ubuf.at[q, zs, at, :], out_hbm.at[dev(zs, y, c), at, :], usem_s.at[q, zs * R + j]
        )

    def expand(zs, j):
        part = pl.ds(*parts[j])
        for i in (1, 2, 0, 3) if planes == 4 else range(planes):
            p = (me + i + 1) % planes
            at = pl.ds(pl.multiple_of((z * planes + p) * rows, 16), rows)
            ubuf[p, zs, part, :] = lax.dot_general(
                rt[zs, part, :], ball[at, :], NT, preferred_element_type=jnp.float32
            ).astype(jnp.bfloat16)
            if i < planes - 1:
                u_copy(p, zs, j).start()
            else:
                u_local(zs, j).start()

    for j in range(R):
        at = pl.ds(*parts[j])
        low = jnp.dot(ctall[at, :], ptall[...], preferred_element_type=jnp.float32)
        moment_next = 0.9 * mom[at, :] + 0.1 * low
        second_next = 0.999 * sec[at, :] + 0.001 * low * low
        mom[at, :] = moment_next
        sec[at, :] = second_next
        ratio = moment_next / (jnp.sqrt(second_next) + 1e-08)
        rt[z, at, :] = ratio.astype(jnp.bfloat16)
        line_start(rat, rsem, j)
        adam_copy(0, j).start()
        adam_copy(1, j).start()

    for j in range(R):
        expand(z, j)

    @pl.loop(1, Z)
    def _(k):
        for j in range(R):
            both(k, lambda zs, below: line_take(rat, rsem, zs, below, j))
            both(k, lambda zs, below: expand(zs, j))

    gather_sent(bas, bsem)
    gather_sent(pro, psem)
    for j in range(R):
        line_sent(rat, rsem, j)

    @pl.loop(1, n)
    def _(k):
        cot_copy(k).wait_send()

    for j in range(R):
        adam_copy(0, j).wait()
        adam_copy(1, j).wait()

    @pl.loop(0, Z)
    def _(zs):
        for j in range(R):
            for i in range(1, planes):
                p = (me + i) % planes
                u_copy(p, zs, j).wait_send()
                u_copy(p, zs, j, recv=True).wait_recv()
            u_local(zs, j).wait()


def on_device(n, Z, Y, tokens, cotangent, basis, moment, second_moment):
    T, D = tokens.shape
    rows, rank = basis.shape
    width = moment.shape[1]
    R = len(parts_of(width))
    bf = jnp.bfloat16
    inside = width % 16 == 0
    ct = cotangent if inside else cotangent.T.reshape(n, width, T)
    any_spec = pl.BlockSpec(memory_space=pl.ANY)
    dma = pltpu.SemaphoreType.DMA
    out, moment_next, second_next = pl.pallas_call(
        functools.partial(kernel, n, Z, Y),
        out_shape=(
            jax.ShapeDtypeStruct((n, width, rows), bf),
            jax.ShapeDtypeStruct((width, rank), jnp.float32),
            jax.ShapeDtypeStruct((width, rank), jnp.float32),
        ),
        in_specs=[any_spec] * 5,
        out_specs=(any_spec,) * 3,
        scratch_shapes=[
            pltpu.VMEM((T, D), bf),
            pltpu.VMEM((D, rank), bf),
            pltpu.VMEM((T, rank), jnp.float32),
            pltpu.VMEM((n * T, rank), bf),
            pltpu.VMEM((width, n * T), bf),
            pltpu.VMEM((width, rank), jnp.float32),
            pltpu.VMEM((width, rank), jnp.float32),
            pltpu.VMEM((Z, width, rank), bf),
            pltpu.VMEM((Y * CORES, Z, width, rows), bf),
            pltpu.VMEM((T, n * width) if inside else (16, 128), bf),
            pltpu.VMEM((n * width, T) if inside else (16, 128), bf),
            dma((6,)),
            dma((2, R)),
            dma((7 + Y, Z)),
            dma((7 + Y, Z)),
            dma((n,)),
            dma((n,)),
            dma((Y * CORES, Z * R)),
            dma((Y * CORES, Z * R)),
            dma((6, Z * R)),
        ],
        compiler_params=pltpu.CompilerParams(
            collective_id=0, has_side_effects=True, vmem_limit_bytes=60 * 2**20
        ),
        cost_estimate=pl.CostEstimate(
            flops=2 * T * rank * (D + n * width) + 2 * rank * rows * n * width,
            bytes_accessed=4 * D * rank, transcendentals=rank * width,
        ),
    )(tokens, ct, basis, moment.T, second_moment.T)
    update = out.reshape(n * width, rows).T
    return (update, moment_next.T, second_next.T)


def solution(mesh):
    n = mesh.shape["rep"]
    Y = max(1, 4 // mesh.shape["groups"])
    Z = n // (Y * CORES)
    in_specs = (
        P(("groups", "rep"), None),
        P(("groups", "rep"), None),
        P("rep", None),
        P(None, "rep"),
        P(None, "rep"),
    )
    out_specs = (P(("groups", "rep"), None), P("groups", "rep"), P("groups", "rep"))
    return jax.shard_map(
        functools.partial(on_device, n, Z, Y),
        mesh=mesh, in_specs=in_specs, out_specs=out_specs, check_vma=False,
    )
```
